128 devices in a mesh: row: 8 (over y_lo, x), col: 16 (over y_hi, z, core).
Axes of the slice: x: 4, y: 4 (y_hi: 2, y_lo: 2; y = y_hi * 2 + y_lo), z: 4, core: 2. Of those that a mesh axis runs over, the one named last changes fastest.
Arguments:
- pair: float32 [512, 512, 128], P('row', 'col'), may hold values from -6 to 6
- single: bfloat16 [512, 384], P(('row', 'col')), may hold values from -6 to 6
- token_valid: int32 [512], replicated, may hold values 0 or 1
- chain_id: int32 [512], replicated, may hold values from 0 to 3, never falling along the last dimension, each value on 1 to 256 neighbouring positions
- w_tri_in: bfloat16 [128, 512], replicated, may hold values from -0.5 to 0.5
- w_tri_gate: bfloat16 [128, 128], replicated, may hold values from -0.5 to 0.5
- w_tri_out: bfloat16 [128, 128], replicated, may hold values from -0.5 to 0.5
- w_att_in: bfloat16 [128, 512], replicated, may hold values from -0.5 to 0.5
- w_att_bias: bfloat16 [128, 4], replicated, may hold values from -6 to 6
- w_att_out: bfloat16 [128, 128], replicated, may hold values from -0.5 to 0.5
- w_single_in: bfloat16 [384, 1536], replicated, may hold values from -0.3125 to 0.3125
- w_pair_bias: bfloat16 [128, 16], replicated, may hold values from -6 to 6
- w_single_out: bfloat16 [384, 384], replicated, may hold values from -0.3125 to 0.3125
Outputs:
- pair_out: float32 [512, 512, 128], P('row', 'col')
- single_out: float32 [512, 384], P(('row', 'col'))
The draws below stay inside these ranges and needn't reach their ends.
All inputs are finite; a program needn't handle non-finite values.
Results may differ from the reference program's by a relative error of at most 0.034.
Values may be sent and summed in bfloat16 or wider, within the bound.
A program may use at most 128 MiB of HBM per device.

```python
import math
import jax
import jax.numpy as jnp
import numpy as np
from jax import lax

C = 128
SINGLE_CHANNELS = 384
H = 4
DH = 32
SINGLE_HEADS = 16
TOKEN_COUNT = 512
BJ = 32
HD = 128
SINGLE_HEAD_DIM = 24


def column_scaled(key, rows, cols, low, high):
    base_key, scale_key = jax.random.split(key)
    base = jax.random.uniform(base_key, (rows, cols), jnp.float32, -1.0, 1.0)
    scales = jnp.exp(jax.random.uniform(scale_key, (cols,), jnp.float32, math.log(low), math.log(high)))
    return base * scales[None, :]


def draw_w_att_bias(key, part):
    key = jax.random.fold_in(key, 11)
    table = column_scaled(key, C, H, 0.5, 3.0)
    return table.astype(jnp.bfloat16)


def draw_w_pair_bias(key, part):
    key = jax.random.fold_in(key, 12)
    table = column_scaled(key, C, SINGLE_HEADS, 0.5, 3.0)
    return table.astype(jnp.bfloat16)


def place_ends(drawn, stream_key, smallest, high):
    spot = [jax.random.randint(jax.random.fold_in(stream_key, axis), (), 0, length) for axis, length in enumerate(drawn.shape)]
    widest = drawn.shape.index(max(drawn.shape))
    beside = spot[:widest] + [(spot[widest] + 1) % drawn.shape[widest]] + spot[widest + 1:]
    return drawn.at[tuple(spot)].set(smallest).at[tuple(beside)].set(high)


def block_scale(key, shape, pieces, low, high):
    gain = 1.0
    for dim, blocks in pieces:
        draws = jax.random.uniform(jax.random.fold_in(jax.random.fold_in(key, 6), dim), (blocks,), jnp.float32, low / len(pieces), high / len(pieces))
        gain = gain * jnp.repeat(jnp.exp(draws), shape[dim] // blocks).reshape((-1,) + (1,) * (len(shape) - 1 - dim))
    return gain


def profile(amount, total, limit, lean):
    weights = [(1 << 20) // math.isqrt(rank ** lean) + 1 for rank in range(2, amount + 1)]
    rest, holding = total - limit - (amount - 1), [1] * (amount - 1)
    while rest > 0:
        movable = [i for i in range(amount - 1) if holding[i] < limit]
        whole, budget = sum([weights[i] for i in movable]), rest
        for i in movable:
            extra = min(limit - holding[i], max(1, budget * weights[i] // whole), rest)
            holding[i] = holding[i] + extra
            rest = rest - extra
    return np.array([limit] + holding)


def uneven(key, count, total, bound, lean):
    if count == 2:
        one = jax.random.randint(key, (), max(1, total - bound), min(bound, total - 1) + 1)
        return jnp.stack([one, total - one])
    tallies = jnp.asarray(profile(count, total, bound, lean), jnp.int32)
    pairs = (count - 1) // 2
    giver, taker = tallies[1:1 + 2 * pairs:2], tallies[2:2 + 2 * pairs:2]
    room = jnp.minimum(giver - 1, bound - taker)
    shifted = jax.random.randint(jax.random.fold_in(key, 1), (pairs,), 0, 1 << 20) % (room + 1)
    tallies = tallies.at[1:1 + 2 * pairs:2].set(giver - shifted).at[2:2 + 2 * pairs:2].set(taker + shifted)
    return tallies[jax.random.permutation(jax.random.fold_in(key, 2), count)]


def normal_values(key, dims, deviation, bound, pieces=(), kind=jnp.bfloat16):
    factor_of = block_scale(key, dims, pieces, -0.22, 0.18) if pieces else 1.0
    result = jax.random.normal(key, dims, jnp.float32) * deviation * factor_of
    return jnp.minimum(jnp.maximum(result, -bound), bound).astype(kind)


def setup_inputs(seed: int = 0) -> dict:
    seeds = jax.random.split(jax.random.key(seed), 14)
    return {
        "pair": normal_values(seeds[0], (TOKEN_COUNT, TOKEN_COUNT, C), 1.0, 6.0, ((0, 8), (1, 16)), jnp.float32),
        "single": normal_values(seeds[1], (TOKEN_COUNT, SINGLE_CHANNELS), 1.0, 6.0, ((0, 128),)),
        "token_valid": place_ends((jax.random.randint(seeds[2], (TOKEN_COUNT,), 0, 8) < 7).astype(jnp.int32), jax.random.fold_in(seeds[2], 1), 0, 1),
        "chain_id": jnp.searchsorted(jnp.cumsum(uneven(seeds[3], 4, TOKEN_COUNT, TOKEN_COUNT // 2, 0)), jnp.arange(TOKEN_COUNT), side="right").astype(jnp.int32),
        "w_tri_in": normal_values(seeds[4], (C, 4 * C), C ** -0.5, 0.5),
        "w_tri_gate": normal_values(seeds[5], (C, C), C ** -0.5, 0.5),
        "w_tri_out": normal_values(seeds[6], (C, C), C ** -0.5, 0.5),
        "w_att_in": normal_values(seeds[7], (C, 4 * HD), C ** -0.5, 0.5),
        "w_att_bias": draw_w_att_bias(jax.random.fold_in(seeds[13], 71), 0),
        "w_att_out": normal_values(seeds[9], (HD, C), HD ** -0.5, 0.5),
        "w_single_in": normal_values(seeds[10], (SINGLE_CHANNELS, 4 * SINGLE_CHANNELS), SINGLE_CHANNELS ** -0.5, 0.3125),
        "w_pair_bias": draw_w_pair_bias(jax.random.fold_in(seeds[13], 71), 0),
        "w_single_out": normal_values(seeds[12], (SINGLE_CHANNELS, SINGLE_CHANNELS), SINGLE_CHANNELS ** -0.5, 0.3125),
    }


def layer_norm(values):
    center = values - lax.optimization_barrier(jnp.mean(values, axis=-1, keepdims=True))
    spread = lax.optimization_barrier(jnp.mean(center * center, axis=-1, keepdims=True))
    return center * lax.rsqrt(spread + 1e-05)

def broaden_rows(values):
    return lax.optimization_barrier(values).astype(jnp.float32)

def project(normed, weight):
    channel_width = normed.shape[-1]
    flat = jnp.dot(normed.reshape(-1, channel_width), weight, preferred_element_type=jnp.float32)
    return flat.reshape(normed.shape[:-1] + (weight.shape[1],))

def reference(pair, single, token_valid, chain_id, w_tri_in, w_tri_gate, w_tri_out, w_att_in, w_att_bias, w_att_out, w_single_in, w_pair_bias, w_single_out):
    valid = token_valid.astype(jnp.float32)
    normed = layer_norm(pair).astype(jnp.bfloat16)
    tri_proj = project(normed, w_tri_in)
    pair_mask = (valid[:, None] * valid[None, :])[:, :, None]
    left = (jax.nn.sigmoid(tri_proj[..., 0:C]) * tri_proj[..., C:2 * C] * pair_mask).astype(jnp.bfloat16)
    right = (jax.nn.sigmoid(tri_proj[..., 2 * C:3 * C]) * tri_proj[..., 3 * C:4 * C] * pair_mask).astype(jnp.bfloat16)
    product = jnp.einsum('ikc,jkc->ijc', broaden_rows(left), broaden_rows(right), precision=lax.Precision.HIGHEST)
    gated = jax.nn.sigmoid(project(normed, w_tri_gate))
    after_mult = pair + gated * project(layer_norm(product).astype(jnp.bfloat16), w_tri_out)
    att_norm = layer_norm(after_mult).astype(jnp.bfloat16)
    att_proj = project(att_norm, w_att_in)
    queries = att_proj[..., 0:HD].astype(jnp.bfloat16).reshape(TOKEN_COUNT, TOKEN_COUNT, H, DH)
    keys_all = att_proj[..., HD:2 * HD].astype(jnp.bfloat16).reshape(TOKEN_COUNT, TOKEN_COUNT, H, DH)
    values_all = att_proj[..., 2 * HD:3 * HD].astype(jnp.bfloat16).reshape(TOKEN_COUNT, TOKEN_COUNT, H, DH)
    att_gate = att_proj[..., 3 * HD:4 * HD]
    tri_bias = project(att_norm, w_att_bias)
    bias_hik = jnp.transpose(tri_bias, (2, 1, 0))
    key_mask = (valid - 1.0) * 10000.0

    def column_block(block):
        first = (block * BJ).astype(jnp.int32)
        query_blk = broaden_rows(lax.dynamic_slice_in_dim(queries, first, BJ, 1))
        key_blk = broaden_rows(lax.dynamic_slice_in_dim(keys_all, first, BJ, 1))
        value_blk = lax.dynamic_slice_in_dim(values_all, first, BJ, 1)
        logit_scores = jnp.einsum('ijhd,kjhd->jhik', query_blk, key_blk) / math.sqrt(DH)
        logit_scores = logit_scores + bias_hik[None] + key_mask
        peak = lax.optimization_barrier(jnp.max(logit_scores, axis=-1, keepdims=True))
        expo = jnp.exp(logit_scores - peak)
        mass = lax.optimization_barrier(jnp.sum(expo, axis=-1))
        summed = jnp.einsum('jhik,kjhd->jhid', broaden_rows(expo.astype(jnp.bfloat16)), broaden_rows(value_blk))
        return jnp.transpose(summed / mass[..., None], (2, 0, 1, 3))
    blocks = lax.map(column_block, jnp.arange(TOKEN_COUNT // BJ, dtype=jnp.int32))
    attended = jnp.transpose(blocks, (1, 0, 2, 3, 4)).reshape(TOKEN_COUNT, TOKEN_COUNT, HD)
    tri_out = (jax.nn.sigmoid(att_gate) * attended).astype(jnp.bfloat16)
    pair_out = after_mult + project(tri_out, w_att_out)
    single_norm = layer_norm(single.astype(jnp.float32)).astype(jnp.bfloat16)
    single_projected = project(single_norm, w_single_in)
    single_query_rows = single_projected[:, 0:SINGLE_CHANNELS].astype(jnp.bfloat16).reshape(TOKEN_COUNT, SINGLE_HEADS, SINGLE_HEAD_DIM)
    single_key_rows = single_projected[:, SINGLE_CHANNELS:2 * SINGLE_CHANNELS].astype(jnp.bfloat16).reshape(TOKEN_COUNT, SINGLE_HEADS, SINGLE_HEAD_DIM)
    svalues = single_projected[:, 2 * SINGLE_CHANNELS:3 * SINGLE_CHANNELS].astype(jnp.bfloat16).reshape(TOKEN_COUNT, SINGLE_HEADS, SINGLE_HEAD_DIM)
    single_gate = single_projected[:, 3 * SINGLE_CHANNELS:4 * SINGLE_CHANNELS]
    pair_bias = project(layer_norm(pair_out).astype(jnp.bfloat16), w_pair_bias)
    allowed = (chain_id[:, None] == chain_id[None, :]) & (token_valid[None, :] == 1)
    mask_add = jnp.where(allowed, 0.0, -10000.0).astype(jnp.float32)
    logit_scores = jnp.einsum('abl,fbl->baf', broaden_rows(single_query_rows), broaden_rows(single_key_rows)) / math.sqrt(SINGLE_HEAD_DIM)
    logit_scores = logit_scores + jnp.transpose(pair_bias, (2, 0, 1)) + mask_add[None]
    peak = lax.optimization_barrier(jnp.max(logit_scores, axis=-1, keepdims=True))
    expo = jnp.exp(logit_scores - peak)
    mass = lax.optimization_barrier(jnp.sum(expo, axis=-1))
    summed = jnp.einsum('hij,jhd->hid', broaden_rows(expo.astype(jnp.bfloat16)), broaden_rows(svalues))
    attended_single = jnp.transpose(summed / mass[..., None], (1, 0, 2)).reshape(TOKEN_COUNT, SINGLE_CHANNELS)
    gated_single = (jax.nn.sigmoid(single_gate) * attended_single).astype(jnp.bfloat16)
    single_out = single.astype(jnp.float32) + jnp.dot(gated_single, w_single_out, preferred_element_type=jnp.float32)
    return (pair_out, single_out)
```

```python
import math

import jax
import jax.numpy as jnp
from jax import lax
from jax.experimental import pallas as pl
from jax.experimental.pallas import tpu as pltpu
from jax.sharding import PartitionSpec as P

MESH = pl.DeviceIdType.MESH
F32 = jnp.float32
BF16 = jnp.bfloat16
ROWS = 8
COLS = 16
DEVICES = ROWS * COLS
LOG2E = math.log2(math.e)
EPS = 1e-05


def norm_down(values):
    mean = jnp.mean(values, axis=0, keepdims=True)
    center = values - mean
    spread = jnp.mean(center * center, axis=0, keepdims=True) + EPS
    return center * lax.rsqrt(spread), mean, jnp.sqrt(spread)


def norm_across(values):
    center = values - jnp.mean(values, axis=-1, keepdims=True)
    spread = jnp.mean(center * center, axis=-1, keepdims=True)
    return center * lax.rsqrt(spread + EPS)


def dot(a, b):
    return jnp.dot(a, b, preferred_element_type=F32)


def join_halves(a, b, half):
    first = lax.broadcasted_iota(jnp.int32, a.shape, 1) < 64
    if half == 0:
        return jnp.where(first, a, pltpu.roll(b, 64, 1))
    return jnp.where(first, pltpu.roll(a, 64, 1), b)


def pair_kernel(
    pair_ref,
    single_ref,
    valid_ref,
    chain_ref,
    valid_smem,
    chain_smem,
    w_tri_in_ref,
    w_tri_gate_ref,
    w_tri_out_ref,
    w_att_in_ref,
    w_att_bias_ref,
    w_att_out_ref,
    w_pair_bias_ref,
    w_single_in_ref,
    w_single_out_ref,
    out_ref,
    single_out_ref,
    w_in_t,
    w_gate_t,
    w_out_t,
    w_key_t,
    scr_a,
    scr_b,
    lr_send,
    lr_recv,
    norm_send,
    norm_recv,
    stat_send,
    stat_recv,
    prod_send,
    prod_recv,
    bias_send,
    bias_recv,
    bias_full,
    query_scr,
    key_scr,
    value_scr,
    gate_scr,
    delta_scr,
    delta_send,
    delta_recv,
    pb_send,
    pb_recv,
    single_send,
    single_recv,
    single_scr,
    single_keys,
    single_values,
    lr_sems,
    norm_sems,
    stat_sems,
    prod_sems,
    bias_sems,
    delta_sems,
    pb_sems,
    single_sems,
):
    row, col = lax.axis_index("row"), lax.axis_index("col")
    me = row * COLS + col
    group = col * ROWS + row

    barrier = pltpu.get_barrier_semaphore()

    def greet(step, carry):
        peer = lax.rem(me + step, DEVICES)
        pl.semaphore_signal(
            barrier,
            inc=1,
            device_id=(peer // COLS, lax.rem(peer, COLS)),
            device_id_type=MESH,
        )
        return carry

    lax.fori_loop(1, DEVICES, greet, 0)

    w_in_t[...] = jnp.transpose(w_tri_in_ref[...].astype(F32)).astype(BF16)
    w_gate_t[...] = jnp.transpose(w_tri_gate_ref[...].astype(F32)).astype(BF16)
    w_out_t[...] = jnp.transpose(w_tri_out_ref[...].astype(F32)).astype(BF16)
    w_key_t[...] = jnp.transpose(w_att_in_ref[:, 128:256].astype(F32)).astype(BF16)

    lane = lax.broadcasted_iota(jnp.int32, (1, 128), 1)
    valid_pick = valid_ref[pl.ds(row // 2, 1), :].astype(F32)
    valid_row = jnp.where(
        (lane // 64) == lax.rem(row, 2), valid_pick, pltpu.roll(valid_pick, 64, 1)
    )
    for t in range(3):
        single_scr[4 * t : 4 * t + 4, :] = single_ref[:, 128 * t : 128 * t + 128].astype(F32)
    single_scr[12:16, :] = jnp.zeros((4, 128), F32)
    single_send[...] = single_scr[0:16, :].astype(BF16)

    def project_block(step, carry):
        picks = [pair_ref[pl.ds(4 * step + a, 64, stride=32), :] for a in range(4)]
        turned = jnp.transpose(jnp.concatenate(picks, axis=0))
        normed, mean, deviation = norm_down(turned)
        normed = normed.astype(BF16)
        norm_send[step] = normed
        stat_send[step] = jnp.concatenate(
            [jnp.broadcast_to(mean, (4, 256)), jnp.broadcast_to(deviation, (4, 256))], axis=0
        )
        proj = dot(w_in_t[...], normed)
        masks = []
        for s in range(2):
            at = col * 32 + 4 * step + 2 * s
            pick = jnp.where(lane < 64, valid_smem[at], valid_smem[at + 1])
            masks.append(valid_row * pick.astype(F32))
        mask = jnp.concatenate(masks, axis=1)
        left = jax.nn.sigmoid(proj[0:128]) * proj[128:256] * mask
        right = jax.nn.sigmoid(proj[256:384]) * proj[384:512] * mask
        for s in range(2):
            scr_a[pl.ds(2 * step + s, 128, stride=16), :] = left[:, s * 128 : (s + 1) * 128]
            scr_b[pl.ds(2 * step + s, 128, stride=16), :] = right[:, s * 128 : (s + 1) * 128]
        return carry

    lax.fori_loop(0, 8, project_block, 0)
    lr_send[:, 0:16, :] = scr_a[...].reshape(128, 16, 128).astype(BF16)
    lr_send[:, 16:32, :] = scr_b[...].reshape(128, 16, 128).astype(BF16)

    pl.semaphore_wait(barrier, DEVICES - 1)

    def send_lr(step, carry):
        peer = lax.rem(me + step, DEVICES)
        pltpu.make_async_remote_copy(
            src_ref=lr_send.at[peer],
            dst_ref=lr_recv.at[me],
            send_sem=lr_sems.at[0],
            recv_sem=lr_sems.at[1],
            device_id=(peer // COLS, lax.rem(peer, COLS)),
            device_id_type=MESH,
        ).start()
        return carry

    lax.fori_loop(1, DEVICES, send_lr, 0)
    lr_recv[pl.ds(me, 1)] = lr_send[pl.ds(me, 1)]

    def send_single(step, carry):
        peer = lax.rem(me + step, DEVICES)
        pltpu.make_async_remote_copy(
            src_ref=single_send,
            dst_ref=single_recv.at[me],
            send_sem=single_sems.at[0],
            recv_sem=single_sems.at[1],
            device_id=(peer // COLS, lax.rem(peer, COLS)),
            device_id_type=MESH,
        ).start()
        return carry

    lax.fori_loop(1, DEVICES, send_single, 0)
    single_recv[me] = single_send[...]

    def send_norm(step, carry):
        peer = lax.rem(row + step, ROWS)
        for sent, received, sems in (
            (norm_send, norm_recv, norm_sems),
            (stat_send, stat_recv, stat_sems),
        ):
            pltpu.make_async_remote_copy(
                src_ref=sent.at[peer],
                dst_ref=received.at[row],
                send_sem=sems.at[0],
                recv_sem=sems.at[1],
                device_id=(peer, col),
                device_id_type=MESH,
            ).start()
        return carry

    lax.fori_loop(1, ROWS, send_norm, 0)
    norm_recv[pl.ds(row, 1)] = norm_send[pl.ds(row, 1)]
    stat_recv[pl.ds(row, 1)] = stat_send[pl.ds(row, 1)]

    rest = pl.ds(0, DEVICES - 1)
    pltpu.make_async_copy(lr_send.at[rest], lr_recv.at[rest], lr_sems.at[1]).wait()
    left_halves, right_halves = [[], []], [[], []]
    for q in range(4):
        for half in range(2):
            for halves, first in ((left_halves, 0), (right_halves, 16)):
                a = lr_recv[32 * q : 32 * q + 16, first : first + 16, :].reshape(256, 128)
                b = lr_recv[32 * q + 16 : 32 * q + 32, first : first + 16, :].reshape(256, 128)
                halves[half].append(join_halves(a.astype(F32), b.astype(F32), half))
    left_t = jnp.concatenate(
        [jnp.concatenate(left_halves[h], axis=1) for h in range(2)], axis=0
    ).astype(BF16)
    right_t = jnp.concatenate(
        [jnp.concatenate(right_halves[h], axis=1) for h in range(2)], axis=0
    )
    right_all = jnp.transpose(right_t).astype(BF16)
    product = dot(right_all, left_t)
    for ib in range(4):
        scr_a[pl.ds(ib, 512, stride=4), :] = product[:, ib * 128 : (ib + 1) * 128]
    prod_send[...] = scr_a[...].reshape(128, 16, 128).astype(BF16)

    def send_product(step, carry):
        peer = lax.rem(me + step, DEVICES)
        peer_row, peer_col = peer // COLS, lax.rem(peer, COLS)
        pltpu.make_async_remote_copy(
            src_ref=prod_send.at[peer_col * ROWS + peer_row],
            dst_ref=prod_recv.at[me],
            send_sem=prod_sems.at[0],
            recv_sem=prod_sems.at[1],
            device_id=(peer_row, peer_col),
            device_id_type=MESH,
        ).start()
        return carry

    lax.fori_loop(1, DEVICES, send_product, 0)
    prod_recv[pl.ds(me, 1)] = prod_send[pl.ds(group, 1)]

    seven = pl.ds(0, ROWS - 1)
    pltpu.make_async_copy(norm_send.at[seven], norm_recv.at[seven], norm_sems.at[1]).wait()
    pltpu.make_async_copy(stat_send.at[seven], stat_recv.at[seven], stat_sems.at[1]).wait()
    pltpu.make_async_copy(prod_send.at[rest], prod_recv.at[rest], prod_sems.at[1]).wait()

    scr_b[...] = prod_recv[...].reshape(2048, 128).astype(F32)
    w_qvg = jnp.concatenate(
        [w_att_in_ref[:, 0:128], w_att_in_ref[:, 256:512]], axis=1
    )
    valid_all = jnp.concatenate([valid_ref[a : a + 1, :] for a in range(4)], axis=1)
    key_mask = (valid_all.astype(F32) - 1.0) * 10000.0
    for jj in range(4):
        at = slice(64 * (jj // 2) * 2, 64 * (jj // 2) * 2 + 128)
        half = jj % 2
        normed = jnp.concatenate(
            [
                join_halves(
                    norm_recv[2 * ib, :, at].astype(F32),
                    norm_recv[2 * ib + 1, :, at].astype(F32),
                    half,
                )
                for ib in range(4)
            ],
            axis=1,
        )
        stats = jnp.concatenate(
            [
                join_halves(stat_recv[2 * ib, :, at], stat_recv[2 * ib + 1, :, at], half)
                for ib in range(4)
            ],
            axis=1,
        )
        received = jnp.concatenate(
            [scr_b[pl.ds(4 * jj + ib, 128, stride=16), :] for ib in range(4)], axis=1
        )
        product_norm, _, _ = norm_down(received)
        gate = jax.nn.sigmoid(dot(w_gate_t[...], normed.astype(BF16)))
        change = gate * dot(w_out_t[...], product_norm.astype(BF16))
        after = normed * stats[4:5] + stats[0:1] + change
        att_t, _, _ = norm_down(after)
        att_bf = att_t.astype(BF16)
        bias = lax.dot_general(
            w_att_bias_ref[...], att_bf, (((1,), (0,)), ((), ())), preferred_element_type=F32
        )
        bias = bias + key_mask
        bias = (bias - jnp.max(bias, axis=1, keepdims=True)) * LOG2E
        for kb in range(4):
            scr_a[pl.ds(4 * jj + kb, 4, stride=16), :] = bias[0:4, kb * 128 : (kb + 1) * 128]
        key_scr[jj] = dot(w_key_t[...], att_bf).astype(BF16)
        att_tok = jnp.transpose(att_t).astype(BF16)
        qvg = dot(att_tok, w_qvg)
        query_scr[jj] = (qvg[:, 0:128] * (LOG2E / math.sqrt(32.0))).astype(BF16)
        value_scr[jj, :, 0:128] = qvg[:, 128:256].astype(BF16)
        value_scr[jj, :, 128:256] = jnp.ones((512, 128), BF16)
        gate_scr[jj] = jax.nn.sigmoid(qvg[:, 256:384])
        delta_scr[jj] = jnp.transpose(change)
    bias_send[...] = scr_a[0:64, :].astype(BF16)

    def send_bias(step, carry):
        peer = lax.rem(me + step, DEVICES)
        pltpu.make_async_remote_copy(
            src_ref=bias_send,
            dst_ref=bias_recv.at[group],
            send_sem=bias_sems.at[0],
            recv_sem=bias_sems.at[1],
            device_id=(peer // COLS, lax.rem(peer, COLS)),
            device_id_type=MESH,
        ).start()
        return carry

    lax.fori_loop(1, DEVICES, send_bias, 0)
    bias_recv[group] = bias_send[...]

    pltpu.make_async_copy(single_recv.at[rest], single_recv.at[rest], single_sems.at[1]).wait()
    scr_b[...] = single_recv[...].reshape(2048, 128).astype(F32)
    for t in range(3):
        for a in range(4):
            single_scr[pl.ds(512 * t + a, 128, stride=4), :] = scr_b[
                pl.ds(4 * t + a, 128, stride=16), :
            ]
    single_all = jnp.concatenate(
        [single_scr[512 * t : 512 * t + 512, :] for t in range(3)], axis=1
    )
    single_norm = norm_across(single_all).astype(BF16)
    single_keys[...] = dot(single_norm, w_single_in_ref[:, 384:768]).astype(BF16)
    single_values[...] = dot(single_norm, w_single_in_ref[:, 768:1152]).astype(BF16)

    pltpu.make_async_copy(bias_recv.at[rest], bias_recv.at[rest], bias_sems.at[1]).wait()

    for h in range(4):
        scr_b[...] = bias_recv[:, 16 * h : 16 * h + 16, :].reshape(2048, 128).astype(F32)
        for kb in range(4):
            bias_full[h, :, kb * 128 : (kb + 1) * 128] = scr_b[pl.ds(kb, 512, stride=4), :]

    def attend(jj, carry):
        keys = key_scr[jj]
        down = lax.broadcasted_iota(jnp.int32, (128, 512), 0)
        head_keys = [
            jnp.where((down >= 32 * h) & (down < 32 * h + 32), keys.astype(F32), 0.0).astype(BF16)
            for h in range(4)
        ]
        across = lax.broadcasted_iota(jnp.int32, (128, 128), 1)
        for ib in range(4):
            span = slice(128 * ib, 128 * ib + 128)
            queries = query_scr[jj, span, :]
            attended = jnp.zeros((128, 128), F32)
            for h in range(4):
                scores = dot(queries, head_keys[h]) + bias_full[h, span, :]
                weights = jnp.exp2(scores - jnp.max(scores, axis=1, keepdims=True)).astype(BF16)
                summed = dot(weights, value_scr[jj])
                attended = jnp.where(
                    (across >= 32 * h) & (across < 32 * h + 32),
                    summed[:, 0:128] / summed[:, 128:256],
                    attended,
                )
            tri_out = (gate_scr[jj, span, :] * attended).astype(BF16)
            delta = delta_scr[jj, span, :] + dot(tri_out, w_att_out_ref[...])
            delta = delta.astype(BF16)
            delta_send[2 * ib, pl.ds(jj, 1)] = delta[0:64].reshape(1, 64, 128)
            delta_send[2 * ib + 1, pl.ds(jj, 1)] = delta[64:128].reshape(1, 64, 128)

        def send_delta(step, carry):
            peer = lax.rem(row + step, ROWS)
            pltpu.make_async_remote_copy(
                src_ref=delta_send.at[peer, jj],
                dst_ref=delta_recv.at[row, jj],
                send_sem=delta_sems.at[0],
                recv_sem=delta_sems.at[1],
                device_id=(peer, col),
                device_id_type=MESH,
            ).start()
            return carry

        lax.fori_loop(1, ROWS, send_delta, 0)
        return carry

    lax.fori_loop(0, 4, attend, 0)
    delta_recv[pl.ds(row, 1)] = delta_send[pl.ds(row, 1)]
    pltpu.make_async_copy(delta_send.at[seven], delta_recv.at[seven], delta_sems.at[1]).wait()

    def finish(step, carry):
        for jj in range(4):
            at = pl.ds(4 * step + jj, 64, stride=32)
            out_ref[at, :] = pair_ref[at, :] + delta_recv[step, jj].astype(F32)
        return carry

    lax.fori_loop(0, 8, finish, 0)

    def pair_bias(step, carry):
        normed = norm_across(out_ref[pl.ds(pl.multiple_of(256 * step, 256), 256), :]).astype(BF16)
        bias = lax.dot_general(
            w_pair_bias_ref[...], normed, (((1,), (1,)), ((), ())), preferred_element_type=F32
        )
        for s in range(2):
            pb_send[2 * step + s] = bias[:, 128 * s : 128 * s + 128]
        return carry

    lax.fori_loop(0, 8, pair_bias, 0)

    def send_pb(step, carry):
        peer = lax.rem(col + step, COLS)
        pltpu.make_async_remote_copy(
            src_ref=pb_send.at[peer],
            dst_ref=pb_recv.at[col],
            send_sem=pb_sems.at[0],
            recv_sem=pb_sems.at[1],
            device_id=(row, peer),
            device_id_type=MESH,
        ).start()
        return carry

    lax.fori_loop(1, COLS, send_pb, 0)
    pb_recv[pl.ds(col, 1)] = pb_send[pl.ds(col, 1)]
    fifteen = pl.ds(0, COLS - 1)
    pltpu.make_async_copy(pb_send.at[fifteen], pb_recv.at[fifteen], pb_sems.at[1]).wait()

    chain_all = jnp.concatenate([chain_ref[a : a + 1, :] for a in range(4)], axis=1)
    own = single_ref[...].astype(F32)
    own_norm = norm_across(own).astype(BF16)
    queries = dot(own_norm, w_single_in_ref[:, 0:384]).astype(BF16).astype(F32)
    gate = jax.nn.sigmoid(dot(own_norm, w_single_in_ref[:, 1152:1536]))
    head = lax.broadcasted_iota(jnp.int32, (16, 384), 0) * 24
    channel = lax.broadcasted_iota(jnp.int32, (16, 384), 1)
    mine = (channel >= head) & (channel < head + 24)
    stacked = jnp.concatenate(
        [jnp.where(mine, jnp.broadcast_to(queries[a : a + 1], (16, 384)), 0.0) for a in range(4)],
        axis=0,
    ).astype(BF16)
    scores = lax.dot_general(
        stacked, single_keys[...], (((1,), (1,)), ((), ())), preferred_element_type=F32
    ) * (1.0 / math.sqrt(24.0))
    quarter = lax.broadcasted_iota(jnp.int32, (16, 128), 1) // 32
    bias_rows = []
    for a in range(4):
        tiles = []
        for g in range(4):
            tile = jnp.zeros((16, 128), F32)
            for part in range(4):
                piece = pb_recv[4 * g + part]
                shift = (32 * (part - a)) % 128
                if shift:
                    piece = pltpu.roll(piece, shift, 1)
                tile = jnp.where(quarter == part, piece, tile)
            tiles.append(tile)
        allowed = (chain_all == chain_smem[4 * me + a]) & (valid_all == 1)
        bias_rows.append(jnp.concatenate(tiles, axis=1) + jnp.where(allowed, 0.0, -10000.0))
    scores = scores + jnp.concatenate(bias_rows, axis=0)
    expo = jnp.exp(scores - jnp.max(scores, axis=1, keepdims=True))
    mass = jnp.sum(expo, axis=1, keepdims=True)
    summed = dot(expo.astype(BF16), single_values[...]) / mass
    attended = jnp.concatenate(
        [
            jnp.sum(jnp.where(mine, summed[16 * a : 16 * a + 16], 0.0), axis=0, keepdims=True)
            for a in range(4)
        ],
        axis=0,
    )
    single_out_ref[...] = own + dot((gate * attended).astype(BF16), w_single_out_ref[...])

    pltpu.make_async_copy(lr_send.at[rest], lr_recv.at[rest], lr_sems.at[0]).wait()
    pltpu.make_async_copy(norm_send.at[seven], norm_recv.at[seven], norm_sems.at[0]).wait()
    pltpu.make_async_copy(stat_send.at[seven], stat_recv.at[seven], stat_sems.at[0]).wait()
    pltpu.make_async_copy(prod_send.at[rest], prod_recv.at[rest], prod_sems.at[0]).wait()
    pltpu.make_async_copy(bias_recv.at[rest], bias_recv.at[rest], bias_sems.at[0]).wait()
    pltpu.make_async_copy(delta_send.at[seven], delta_recv.at[seven], delta_sems.at[0]).wait()
    pltpu.make_async_copy(pb_send.at[fifteen], pb_recv.at[fifteen], pb_sems.at[0]).wait()
    pltpu.make_async_copy(single_recv.at[rest], single_recv.at[rest], single_sems.at[0]).wait()


def per_device(
    pair,
    single,
    token_valid,
    chain_id,
    w_tri_in,
    w_tri_gate,
    w_tri_out,
    w_att_in,
    w_att_bias,
    w_att_out,
    w_single_in,
    w_pair_bias,
    w_single_out,
):
    vmem = pl.BlockSpec(memory_space=pltpu.VMEM)
    smem = pl.BlockSpec(memory_space=pltpu.SMEM)
    dma = pltpu.SemaphoreType.DMA
    pair_out, single_out = pl.pallas_call(
        pair_kernel,
        out_shape=(
            jax.ShapeDtypeStruct((2048, 128), F32),
            jax.ShapeDtypeStruct((4, 384), F32),
        ),
        in_specs=[vmem] * 4 + [smem] * 2 + [vmem] * 9,
        out_specs=(vmem, vmem),
        scratch_shapes=[
            pltpu.VMEM((512, 128), BF16),
            pltpu.VMEM((128, 128), BF16),
            pltpu.VMEM((128, 128), BF16),
            pltpu.VMEM((128, 128), BF16),
            pltpu.VMEM((2048, 128), F32),
            pltpu.VMEM((2048, 128), F32),
            pltpu.VMEM((128, 32, 128), BF16),
            pltpu.VMEM((128, 32, 128), BF16),
            pltpu.VMEM((8, 128, 256), BF16),
            pltpu.VMEM((8, 128, 256), BF16),
            pltpu.VMEM((8, 8, 256), F32),
            pltpu.VMEM((8, 8, 256), F32),
            pltpu.VMEM((128, 16, 128), BF16),
            pltpu.VMEM((128, 16, 128), BF16),
            pltpu.VMEM((64, 128), BF16),
            pltpu.VMEM((128, 64, 128), BF16),
            pltpu.VMEM((4, 512, 512), F32),
            pltpu.VMEM((4, 512, 128), BF16),
            pltpu.VMEM((4, 128, 512), BF16),
            pltpu.VMEM((4, 512, 256), BF16),
            pltpu.VMEM((4, 512, 128), F32),
            pltpu.VMEM((4, 512, 128), F32),
            pltpu.VMEM((8, 4, 64, 128), BF16),
            pltpu.VMEM((8, 4, 64, 128), BF16),
            pltpu.VMEM((COLS, 16, 128), F32),
            pltpu.VMEM((COLS, 16, 128), F32),
            pltpu.VMEM((16, 128), BF16),
            pltpu.VMEM((128, 16, 128), BF16),
            pltpu.VMEM((1536, 128), F32),
            pltpu.VMEM((512, 384), BF16),
            pltpu.VMEM((512, 384), BF16),
        ]
        + [dma((2,))] * 8,
        compiler_params=pltpu.CompilerParams(
            collective_id=0, has_side_effects=True, vmem_limit_bytes=52 * 1024 * 1024
        ),
    )(
        pair.reshape(2048, 128),
        single,
        token_valid.reshape(4, 128),
        chain_id.reshape(4, 128),
        token_valid,
        chain_id,
        w_tri_in,
        w_tri_gate,
        w_tri_out,
        w_att_in,
        w_att_bias.T,
        w_att_out,
        w_pair_bias.T,
        w_single_in,
        w_single_out,
    )
    return pair_out.reshape(64, 32, 128), single_out


def solution(mesh):
    placed = (P("row", "col", None), P(("row", "col"), None)) + (P(),) * 11
    return jax.shard_map(
        per_device,
        mesh=mesh,
        in_specs=placed,
        out_specs=(P("row", "col", None), P(("row", "col"), None)),
        check_vma=False,
    )
```

```python
import math

import jax
import jax.numpy as jnp
from jax import lax
from jax.experimental import pallas as pl
from jax.experimental.pallas import tpu as pltpu
from jax.sharding import PartitionSpec as P

MESH = pl.DeviceIdType.MESH
F32 = jnp.float32
BF16 = jnp.bfloat16
ROWS = 8
COLS = 16
DEVICES = ROWS * COLS
LOG2E = math.log2(math.e)
EPS = 1e-05


def norm_down(values):
    mean = jnp.mean(values, axis=0, keepdims=True)
    center = values - mean
    spread = jnp.mean(center * center, axis=0, keepdims=True) + EPS
    return center * lax.rsqrt(spread), mean, jnp.sqrt(spread)


def norm_across(values):
    center = values - jnp.mean(values, axis=-1, keepdims=True)
    spread = jnp.mean(center * center, axis=-1, keepdims=True)
    return center * lax.rsqrt(spread + EPS)


def dot(a, b):
    return jnp.dot(a, b, preferred_element_type=F32)


def join_halves(a, b, half):
    first = lax.broadcasted_iota(jnp.int32, a.shape, 1) < 64
    if half == 0:
        return jnp.where(first, a, pltpu.roll(b, 64, 1))
    return jnp.where(first, pltpu.roll(a, 64, 1), b)


def window_kernel(*refs):
    inputs, (out_ref, single_out_ref), scratch = refs[:15], refs[15:17], refs[17:]
    staged, in_sems, scratch = scratch[:15], scratch[15], scratch[16:]
    (
        pair_ref,
        single_ref,
        valid_ref,
        chain_ref,
        valid_smem,
        chain_smem,
        w_tri_in_ref,
        w_tri_gate_ref,
        w_tri_out_ref,
        w_att_in_ref,
        w_att_bias_ref,
        w_att_out_ref,
        w_pair_bias_ref,
        w_single_in_ref,
        w_single_out_ref,
    ) = staged
    (
        w_in_t,
        w_gate_t,
        w_out_t,
        w_key_t,
        w_pair_slots,
        scr_a,
        scr_b,
        lr_send,
        lr_recv,
        norm_send,
        norm_recv,
        stat_send,
        stat_recv,
        prod_send,
        prod_recv,
        bias_send,
        bias_recv,
        bias_full,
        att_t_scr,
        after_scr,
        change_scr,
        query_scr,
        key_scr,
        value_scr,
        gate_scr,
        attended_scr,
        delta_send,
        delta_recv,
        pb_sum,
        pb_send,
        pb_recv,
        single_send,
        single_recv,
        single_scr,
        single_keys,
        single_values,
        lr_sems,
        norm_sems,
        stat_sems,
        prod_sems,
        bias_sems,
        bias_send_sems,
        delta_sems,
        pb_sems,
        single_sems,
    ) = scratch
    loads = [
        pltpu.make_async_copy(inputs[n], staged[n], in_sems.at[n]) for n in range(len(inputs))
    ]
    for load in loads:
        load.start()

    row, col = lax.axis_index("row"), lax.axis_index("col")
    me = row * COLS + col
    group = col * ROWS + row
    core = lax.rem(col, 2)
    partner = col + 1 - 2 * core

    barrier = pltpu.get_barrier_semaphore()

    for row_step in range(ROWS):
        for col_step in range(COLS):
            if row_step or col_step:
                pl.semaphore_signal(
                    barrier,
                    inc=1,
                    device_id=(
                        lax.rem(row + row_step, ROWS),
                        lax.rem(col + col_step, COLS),
                    ),
                    device_id_type=MESH,
                )

    for load in loads:
        load.wait()
    w_in_t[...] = jnp.transpose(w_tri_in_ref[...].astype(F32)).astype(BF16)
    w_gate_t[...] = jnp.transpose(w_tri_gate_ref[...].astype(F32)).astype(BF16)
    w_out_t[...] = jnp.transpose(w_tri_out_ref[...].astype(F32)).astype(BF16)
    lane = lax.broadcasted_iota(jnp.int32, (1, 128), 1)
    valid_pick = valid_ref[pl.ds(row // 2, 1), :].astype(F32)
    valid_row = jnp.where(
        (lane // 64) == lax.rem(row, 2), valid_pick, pltpu.roll(valid_pick, 64, 1)
    )
    for t in range(3):
        single_scr[4 * t : 4 * t + 4, :] = single_ref[:, 128 * t : 128 * t + 128].astype(F32)
    single_scr[12:16, :] = jnp.zeros((4, 128), F32)
    single_send[...] = single_scr[0:16, :].astype(BF16)

    def project_block(step, carry):
        picks = [pair_ref[pl.ds(4 * step + a, 64, stride=32), :] for a in range(4)]
        turned = jnp.transpose(jnp.concatenate(picks, axis=0))
        normed, mean, deviation = norm_down(turned)
        normed = normed.astype(BF16)
        norm_send[step] = normed
        stat_send[step] = jnp.concatenate(
            [jnp.broadcast_to(mean, (4, 256)), jnp.broadcast_to(deviation, (4, 256))], axis=0
        )
        proj = dot(w_in_t[...], normed)
        masks = []
        for s in range(2):
            at = col * 32 + 4 * step + 2 * s
            pick = jnp.where(lane < 64, valid_smem[at], valid_smem[at + 1])
            masks.append(valid_row * pick.astype(F32))
        mask = jnp.concatenate(masks, axis=1)
        left = jax.nn.sigmoid(proj[0:128]) * proj[128:256] * mask
        right = jax.nn.sigmoid(proj[256:384]) * proj[384:512] * mask
        for s in range(2):
            scr_a[pl.ds(2 * step + s, 128, stride=16), :] = left[:, s * 128 : (s + 1) * 128]
            scr_b[pl.ds(2 * step + s, 128, stride=16), :] = right[:, s * 128 : (s + 1) * 128]
        return carry

    lax.fori_loop(0, 8, project_block, 0)
    lr_send[:, 0:16, :] = scr_a[...].reshape(128, 16, 128).astype(BF16)
    lr_send[:, 16:32, :] = scr_b[...].reshape(128, 16, 128).astype(BF16)

    pl.semaphore_wait(barrier, DEVICES - 1)

    def send_lr(step, carry):
        peer = lax.rem(me + step, DEVICES)
        pltpu.make_async_remote_copy(
            src_ref=lr_send.at[peer],
            dst_ref=lr_recv.at[me],
            send_sem=lr_sems.at[0],
            recv_sem=lr_sems.at[1],
            device_id=(peer // COLS, lax.rem(peer, COLS)),
            device_id_type=MESH,
        ).start()
        return carry

    lax.fori_loop(1, DEVICES, send_lr, 0)
    lr_recv[pl.ds(me, 1)] = lr_send[pl.ds(me, 1)]

    def send_single(step, carry):
        peer = lax.rem(row + step, ROWS)
        pltpu.make_async_remote_copy(
            src_ref=single_send,
            dst_ref=single_recv.at[col // 2, core, row],
            send_sem=single_sems.at[0],
            recv_sem=single_sems.at[1],
            device_id=(peer, col),
            device_id_type=MESH,
        ).start()
        return carry

    lax.fori_loop(1, ROWS, send_single, 0)
    single_recv[col // 2, core, row] = single_send[...]

    rest = pl.ds(0, DEVICES - 1)
    pltpu.make_async_copy(lr_send.at[rest], lr_recv.at[rest], lr_sems.at[0]).wait()

    def send_norm(step, carry):
        peer = lax.rem(row + step, ROWS)
        for sent, received, sems in (
            (norm_send, norm_recv, norm_sems),
            (stat_send, stat_recv, stat_sems),
        ):
            pltpu.make_async_remote_copy(
                src_ref=sent.at[peer],
                dst_ref=received.at[row],
                send_sem=sems.at[0],
                recv_sem=sems.at[1],
                device_id=(peer, col),
                device_id_type=MESH,
            ).start()
        return carry

    lax.fori_loop(1, ROWS, send_norm, 0)
    norm_recv[pl.ds(row, 1)] = norm_send[pl.ds(row, 1)]
    stat_recv[pl.ds(row, 1)] = stat_send[pl.ds(row, 1)]

    pltpu.make_async_copy(lr_send.at[rest], lr_recv.at[rest], lr_sems.at[1]).wait()
    left_halves, right_halves = [[], []], [[], []]
    for q in range(4):
        for half in range(2):
            for halves, first in ((left_halves, 0), (right_halves, 16)):
                a = lr_recv[32 * q : 32 * q + 16, first : first + 16, :].reshape(256, 128)
                b = lr_recv[32 * q + 16 : 32 * q + 32, first : first + 16, :].reshape(256, 128)
                halves[half].append(join_halves(a.astype(F32), b.astype(F32), half))
    left_t = jnp.concatenate(
        [jnp.concatenate(left_halves[h], axis=1) for h in range(2)], axis=0
    ).astype(BF16)
    right_t = jnp.concatenate(
        [jnp.concatenate(right_halves[h], axis=1) for h in range(2)], axis=0
    )
    right_all = jnp.transpose(right_t).astype(BF16)
    product = dot(right_all, left_t)
    for ib in range(4):
        scr_a[pl.ds(ib, 512, stride=4), :] = product[:, ib * 128 : (ib + 1) * 128]
    prod_send[...] = scr_a[...].reshape(128, 16, 128).astype(BF16)

    def send_product(step, carry):
        peer = lax.rem(me + step, DEVICES)
        peer_row, peer_col = peer // COLS, lax.rem(peer, COLS)
        pltpu.make_async_remote_copy(
            src_ref=prod_send.at[peer_col * ROWS + peer_row],
            dst_ref=prod_recv.at[me],
            send_sem=prod_sems.at[0],
            recv_sem=prod_sems.at[1],
            device_id=(peer_row, peer_col),
            device_id_type=MESH,
        ).start()
        return carry

    lax.fori_loop(1, DEVICES, send_product, 0)
    prod_recv[pl.ds(me, 1)] = prod_send[pl.ds(group, 1)]

    seven = pl.ds(0, ROWS - 1)
    pltpu.make_async_copy(norm_send.at[seven], norm_recv.at[seven], norm_sems.at[1]).wait()
    pltpu.make_async_copy(stat_send.at[seven], stat_recv.at[seven], stat_sems.at[1]).wait()
    pltpu.make_async_copy(prod_send.at[rest], prod_recv.at[rest], prod_sems.at[1]).wait()

    scr_b[...] = prod_recv[...].reshape(2048, 128).astype(F32)
    valid_all = jnp.concatenate([valid_ref[a : a + 1, :] for a in range(4)], axis=1)
    key_mask = (valid_all.astype(F32) - 1.0) * 10000.0
    for jj in range(4):
        at = slice(64 * (jj // 2) * 2, 64 * (jj // 2) * 2 + 128)
        half = jj % 2
        normed = jnp.concatenate(
            [
                join_halves(
                    norm_recv[2 * ib, :, at].astype(F32),
                    norm_recv[2 * ib + 1, :, at].astype(F32),
                    half,
                )
                for ib in range(4)
            ],
            axis=1,
        )
        stats = jnp.concatenate(
            [
                join_halves(stat_recv[2 * ib, :, at], stat_recv[2 * ib + 1, :, at], half)
                for ib in range(4)
            ],
            axis=1,
        )
        received = jnp.concatenate(
            [scr_b[pl.ds(4 * jj + ib, 128, stride=16), :] for ib in range(4)], axis=1
        )
        product_norm, _, _ = norm_down(received)
        gate = jax.nn.sigmoid(dot(w_gate_t[...], normed.astype(BF16)))
        change = gate * dot(w_out_t[...], product_norm.astype(BF16))
        after = normed * stats[4:5] + stats[0:1] + change
        att_t, _, _ = norm_down(after)
        att_bf = att_t.astype(BF16)
        att_t_scr[jj] = att_bf
        after_scr[jj] = after
        change_scr[jj] = change
        bias = lax.dot_general(
            w_att_bias_ref[...], att_bf, (((1,), (0,)), ((), ())), preferred_element_type=F32
        )
        bias = bias + key_mask
        bias = (bias - jnp.max(bias, axis=1, keepdims=True)) * LOG2E
        for kb in range(4):
            scr_a[pl.ds(4 * jj + kb, 4, stride=16), :] = bias[0:4, kb * 128 : (kb + 1) * 128]
    bias_send[...] = scr_a[0:64, :].reshape(4, 16, 128).astype(BF16)

    def send_bias(slot):
        def push(step, carry):
            peer = lax.rem(me + step, DEVICES)
            pltpu.make_async_remote_copy(
                src_ref=bias_send.at[2 * lax.rem(peer, 2) + slot],
                dst_ref=bias_recv.at[slot, group],
                send_sem=bias_send_sems.at[slot],
                recv_sem=bias_sems.at[slot],
                device_id=(peer // COLS, lax.rem(peer, COLS)),
                device_id_type=MESH,
            ).start()
            return carry

        lax.fori_loop(1, DEVICES, push, 0)
        bias_recv[slot, group] = bias_send[2 * core + slot]

    def bias_left(slot):
        pltpu.make_async_copy(
            bias_recv.at[slot, rest], bias_recv.at[slot, rest], bias_send_sems.at[slot]
        ).wait()

    send_bias(0)

    w_key_t[...] = jnp.transpose(w_att_in_ref[:, 128:256].astype(F32)).astype(BF16)
    w_qvg = jnp.concatenate([w_att_in_ref[:, 0:128], w_att_in_ref[:, 256:512]], axis=1)

    for jj in range(4):
        att_bf = att_t_scr[jj]
        key_scr[jj] = dot(w_key_t[...], att_bf).astype(BF16)
        qvg = dot(jnp.transpose(att_bf.astype(F32)).astype(BF16), w_qvg)
        query_scr[jj] = (qvg[:, 0:128] * (LOG2E / math.sqrt(32.0))).astype(BF16)
        value_scr[jj, :, 0:128] = qvg[:, 128:256].astype(BF16)
        value_scr[jj, :, 128:256] = jnp.ones((512, 128), BF16)
        gate_scr[jj] = jax.nn.sigmoid(qvg[:, 256:384])
    padded = jnp.concatenate(
        [w_pair_bias_ref[...].astype(F32), jnp.zeros((112, 128), F32)], axis=0
    )
    w_pair = jnp.transpose(padded)
    for slot in range(8):
        moved = pltpu.roll(w_pair, 16 * slot, 1) if slot else w_pair
        w_pair_slots[slot] = moved.astype(BF16)
    pb_sum[...] = jnp.zeros((2, 128, 128), F32)

    across = lax.broadcasted_iota(jnp.int32, (128, 128), 1) // 32
    down = lax.broadcasted_iota(jnp.int32, (128, 512), 0) // 32

    def attend(slot, head, begins, ends):
        scr_b[...] = bias_recv[slot].reshape(2048, 128).astype(F32)
        for kb in range(4):
            bias_full[:, kb * 128 : (kb + 1) * 128] = scr_b[pl.ds(kb, 512, stride=4), :]

        for jj in range(4):
            keys = jnp.where(down == head, key_scr[jj].astype(F32), 0.0).astype(BF16)
            if ends:
                after_tok = jnp.transpose(after_scr[jj])
                change_tok = jnp.transpose(change_scr[jj])
            for ib in range(4):
                span = slice(128 * ib, 128 * ib + 128)
                scores = dot(query_scr[jj, span, :], keys) + bias_full[span, :]
                weights = jnp.exp2(scores - jnp.max(scores, axis=1, keepdims=True)).astype(BF16)
                summed = dot(weights, value_scr[jj])
                before = 0.0 if begins else attended_scr[jj, span, :]
                attended = jnp.where(across == head, summed[:, 0:128] / summed[:, 128:256], before)
                if not ends:
                    attended_scr[jj, span, :] = attended
                    continue
                tri_out = (gate_scr[jj, span, :] * attended).astype(BF16)
                added = dot(tri_out, w_att_out_ref[...])
                delta = (change_tok[span] + added).astype(BF16)
                delta_send[2 * ib, pl.ds(jj, 1)] = delta[0:64].reshape(1, 64, 128)
                delta_send[2 * ib + 1, pl.ds(jj, 1)] = delta[64:128].reshape(1, 64, 128)
                scr_a[span, :] = after_tok[span] + added
            if ends:

                def send_delta(step, carry, jj=jj):
                    peer = lax.rem(row + step, ROWS)
                    pltpu.make_async_remote_copy(
                        src_ref=delta_send.at[peer, jj],
                        dst_ref=delta_recv.at[row, jj],
                        send_sem=delta_sems.at[0],
                        recv_sem=delta_sems.at[1],
                        device_id=(peer, col),
                        device_id_type=MESH,
                    ).start()
                    return carry

                lax.fori_loop(1, ROWS, send_delta, 0)
                total = pb_sum[jj // 2]
                for a in range(4):
                    normed = norm_across(scr_a[pl.ds(a, 128, stride=4), :]).astype(BF16)
                    total = total + dot(normed, w_pair_slots[4 * (jj % 2) + a])
                pb_sum[jj // 2] = total

    def hand_on(slot):
        return pltpu.make_async_remote_copy(
            src_ref=bias_recv.at[slot],
            dst_ref=bias_recv.at[2 + slot],
            send_sem=bias_send_sems.at[2 + slot],
            recv_sem=bias_sems.at[2 + slot],
            device_id=(row, partner),
            device_id_type=MESH,
        )

    def gathered(slot):
        pltpu.make_async_copy(
            bias_recv.at[slot, rest], bias_recv.at[slot, rest], bias_sems.at[slot]
        ).wait()

    bias_left(0)
    send_bias(1)
    gathered(0)
    hand_on(0).start()
    pltpu.make_async_copy(
        single_recv.at[0, 0, seven], single_recv.at[0, 0, seven], single_sems.at[1]
    ).wait()

    def spread_single(step, carry):
        peer = lax.rem(col + 2 * step, COLS)
        pltpu.make_async_remote_copy(
            src_ref=single_recv.at[col // 2, core],
            dst_ref=single_recv.at[col // 2, core],
            send_sem=single_sems.at[2],
            recv_sem=single_sems.at[3],
            device_id=(row, peer),
            device_id_type=MESH,
        ).start()
        return carry

    lax.fori_loop(1, COLS // 2, spread_single, 0)
    attend(0, 2 * core, True, False)
    hand_on(0).wait_recv()
    attend(2, 2 * (1 - core), False, False)
    gathered(1)
    hand_on(1).start()
    pltpu.make_async_copy(
        single_recv.at[seven, 0], single_recv.at[seven, 0], single_sems.at[3]
    ).wait()
    pltpu.make_async_remote_copy(
        src_ref=single_recv.at[:, core],
        dst_ref=single_recv.at[:, core],
        send_sem=single_sems.at[4],
        recv_sem=single_sems.at[5],
        device_id=(row, partner),
        device_id_type=MESH,
    ).start()
    attend(1, 2 * core + 1, False, False)
    hand_on(1).wait_recv()
    attend(3, 2 * (1 - core) + 1, False, True)

    for u in range(2):
        pb_send[:, u, :] = pb_sum[u]

    def send_pb(step, carry):
        peer = lax.rem(me + step, DEVICES)
        pltpu.make_async_remote_copy(
            src_ref=pb_send.at[peer],
            dst_ref=pb_recv.at[group],
            send_sem=pb_sems.at[0],
            recv_sem=pb_sems.at[1],
            device_id=(peer // COLS, lax.rem(peer, COLS)),
            device_id_type=MESH,
        ).start()
        return carry

    lax.fori_loop(1, DEVICES, send_pb, 0)
    pb_recv[pl.ds(group, 1)] = pb_send[pl.ds(me, 1)]
    pltpu.make_async_copy(
        single_recv.at[:, core], single_recv.at[:, 1 - core], single_sems.at[5]
    ).wait()
    scr_b[...] = single_recv[...].reshape(2048, 128).astype(F32)
    for t in range(3):
        for a in range(4):
            for r in range(ROWS):
                single_scr[512 * t + 128 * a + 16 * r : 512 * t + 128 * a + 16 * r + 16, :] = scr_b[
                    pl.ds(16 * r + 4 * t + a, 16, stride=128), :
                ]
    single_all = jnp.concatenate(
        [single_scr[512 * t : 512 * t + 512, :] for t in range(3)], axis=1
    )
    single_norm = norm_across(single_all).astype(BF16)
    single_keys[...] = dot(single_norm, w_single_in_ref[:, 384:768]).astype(BF16)
    single_values[...] = dot(single_norm, w_single_in_ref[:, 768:1152]).astype(BF16)

    delta_recv[pl.ds(row, 1)] = delta_send[pl.ds(row, 1)]
    pltpu.make_async_copy(delta_send.at[seven], delta_recv.at[seven], delta_sems.at[1]).wait()

    for k in range(32):
        at = pl.ds(k, 64, stride=32)
        out_ref[at, :] = pair_ref[at, :] + delta_recv[k // 4, k % 4].astype(F32)
    pltpu.make_async_copy(pb_send.at[rest], pb_recv.at[rest], pb_sems.at[1]).wait()

    chain_all = jnp.concatenate([chain_ref[a : a + 1, :] for a in range(4)], axis=1)
    source = lax.broadcasted_iota(jnp.int32, (512, 512), 0)
    place = lax.broadcasted_iota(jnp.int32, (512, 512), 1)
    order = jnp.where(source == 4 * (place % 128) + place // 128, 1.0, 0.0).astype(BF16)
    traits = jnp.concatenate([chain_all, valid_all, jnp.zeros((6, 512), jnp.int32)], axis=0)
    ordered = dot(traits.astype(F32).astype(BF16), order)
    turned = [jnp.transpose(pb_recv[:, u, :]) for u in range(2)]
    pair_bias = jnp.concatenate(
        [turned[jj // 2][64 * (jj % 2) : 64 * (jj % 2) + 64] for jj in range(4)], axis=1
    )
    own = single_ref[...].astype(F32)
    own_norm = norm_across(own).astype(BF16)
    queries = dot(own_norm, w_single_in_ref[:, 0:384]).astype(BF16).astype(F32)
    gate = jax.nn.sigmoid(dot(own_norm, w_single_in_ref[:, 1152:1536]))
    head = lax.broadcasted_iota(jnp.int32, (16, 384), 0) * 24
    channel = lax.broadcasted_iota(jnp.int32, (16, 384), 1)
    mine = (channel >= head) & (channel < head + 24)
    stacked = jnp.concatenate(
        [jnp.where(mine, jnp.broadcast_to(queries[a : a + 1], (16, 384)), 0.0) for a in range(4)],
        axis=0,
    ).astype(BF16)
    scores = lax.dot_general(
        stacked, single_keys[...], (((1,), (1,)), ((), ())), preferred_element_type=F32
    ) * (1.0 / math.sqrt(24.0))
    masks = []
    for a in range(4):
        own_chain = chain_smem[4 * me + a].astype(F32)
        allowed = (ordered[0:1] == own_chain) & (ordered[1:2] == 1.0)
        masks.append(jnp.broadcast_to(jnp.where(allowed, 0.0, -10000.0), (16, 512)))
    scores = scores + pair_bias + jnp.concatenate(masks, axis=0)
    expo = jnp.exp(scores - jnp.max(scores, axis=1, keepdims=True))
    mass = jnp.sum(expo, axis=1, keepdims=True)
    summed = dot(expo.astype(BF16), single_values[...]) / mass
    attended = jnp.concatenate(
        [
            jnp.sum(jnp.where(mine, summed[16 * a : 16 * a + 16], 0.0), axis=0, keepdims=True)
            for a in range(4)
        ],
        axis=0,
    )
    single_out_ref[...] = own + dot((gate * attended).astype(BF16), w_single_out_ref[...])

    pltpu.make_async_copy(norm_send.at[seven], norm_recv.at[seven], norm_sems.at[0]).wait()
    pltpu.make_async_copy(stat_send.at[seven], stat_recv.at[seven], stat_sems.at[0]).wait()
    pltpu.make_async_copy(prod_send.at[rest], prod_recv.at[rest], prod_sems.at[0]).wait()
    bias_left(1)
    for slot in range(2):
        hand_on(slot).wait_send()
    pltpu.make_async_copy(delta_send.at[seven], delta_recv.at[seven], delta_sems.at[0]).wait()
    pltpu.make_async_copy(pb_send.at[rest], pb_recv.at[rest], pb_sems.at[0]).wait()
    pltpu.make_async_copy(
        single_recv.at[0, 0, seven], single_recv.at[0, 0, seven], single_sems.at[0]
    ).wait()
    pltpu.make_async_copy(
        single_recv.at[seven, 0], single_recv.at[seven, 0], single_sems.at[2]
    ).wait()
    pltpu.make_async_copy(
        single_recv.at[:, core], single_recv.at[:, 1 - core], single_sems.at[4]
    ).wait()


def per_device(
    pair,
    single,
    token_valid,
    chain_id,
    w_tri_in,
    w_tri_gate,
    w_tri_out,
    w_att_in,
    w_att_bias,
    w_att_out,
    w_single_in,
    w_pair_bias,
    w_single_out,
):
    vmem = pl.BlockSpec(memory_space=pltpu.VMEM)
    inputs = (
        pair.reshape(2048, 128),
        single,
        token_valid.reshape(4, 128),
        chain_id.reshape(4, 128),
        token_valid,
        chain_id,
        w_tri_in,
        w_tri_gate,
        w_tri_out,
        w_att_in,
        w_att_bias.T,
        w_att_out,
        w_pair_bias.T,
        w_single_in,
        w_single_out,
    )
    dma = pltpu.SemaphoreType.DMA
    staged = [
        pltpu.SMEM(x.shape, x.dtype) if x.ndim == 1 else pltpu.VMEM(x.shape, x.dtype)
        for x in inputs
    ]
    pair_out, single_out = pl.pallas_call(
        window_kernel,
        out_shape=(
            jax.ShapeDtypeStruct((2048, 128), F32),
            jax.ShapeDtypeStruct((4, 384), F32),
        ),
        in_specs=[pl.BlockSpec(memory_space=pltpu.HBM)] * len(inputs),
        out_specs=(vmem, vmem),
        scratch_shapes=staged
        + [
            dma((len(inputs),)),
            pltpu.VMEM((512, 128), BF16),
            pltpu.VMEM((128, 128), BF16),
            pltpu.VMEM((128, 128), BF16),
            pltpu.VMEM((128, 128), BF16),
            pltpu.VMEM((8, 128, 128), BF16),
            pltpu.VMEM((2048, 128), F32),
            pltpu.VMEM((2048, 128), F32),
            pltpu.VMEM((128, 32, 128), BF16),
            pltpu.VMEM((128, 32, 128), BF16),
            pltpu.VMEM((8, 128, 256), BF16),
            pltpu.VMEM((8, 128, 256), BF16),
            pltpu.VMEM((8, 8, 256), F32),
            pltpu.VMEM((8, 8, 256), F32),
            pltpu.VMEM((128, 16, 128), BF16),
            pltpu.VMEM((128, 16, 128), BF16),
            pltpu.VMEM((4, 16, 128), BF16),
            pltpu.VMEM((4, 128, 16, 128), BF16),
            pltpu.VMEM((512, 512), F32),
            pltpu.VMEM((4, 128, 512), BF16),
            pltpu.VMEM((4, 128, 512), F32),
            pltpu.VMEM((4, 128, 512), F32),
            pltpu.VMEM((4, 512, 128), BF16),
            pltpu.VMEM((4, 128, 512), BF16),
            pltpu.VMEM((4, 512, 256), BF16),
            pltpu.VMEM((4, 512, 128), F32),
            pltpu.VMEM((4, 512, 128), F32),
            pltpu.VMEM((8, 4, 64, 128), BF16),
            pltpu.VMEM((8, 4, 64, 128), BF16),
            pltpu.VMEM((2, 128, 128), F32),
            pltpu.VMEM((128, 2, 128), F32),
            pltpu.VMEM((128, 2, 128), F32),
            pltpu.VMEM((16, 128), BF16),
            pltpu.VMEM((8, 2, 8, 16, 128), BF16),
            pltpu.VMEM((1536, 128), F32),
            pltpu.VMEM((512, 384), BF16),
            pltpu.VMEM((512, 384), BF16),
            dma((2,)),
            dma((2,)),
            dma((2,)),
            dma((2,)),
            dma((4,)),
            dma((4,)),
            dma((2,)),
            dma((2,)),
            dma((6,)),
        ],
        compiler_params=pltpu.CompilerParams(
            collective_id=0, has_side_effects=True, vmem_limit_bytes=58 * 1024 * 1024
        ),
    )(*inputs)
    return pair_out.reshape(64, 32, 128), single_out


def solution(mesh):
    placed = (P("row", "col", None), P(("row", "col"), None)) + (P(),) * 11
    return jax.shard_map(
        per_device,
        mesh=mesh,
        in_specs=placed,
        out_specs=(P("row", "col", None), P(("row", "col"), None)),
        check_vma=False,
    )
```

```python
import math

import jax
import jax.numpy as jnp
from jax import lax
from jax.experimental import pallas as pl
from jax.experimental.pallas import tpu as pltpu
from jax.sharding import PartitionSpec as P

MESH = pl.DeviceIdType.MESH
F32 = jnp.float32
BF16 = jnp.bfloat16
ROWS = 8
COLS = 16
DEVICES = ROWS * COLS
LOG2E = math.log2(math.e)
EPS = 1e-05


def norm_down(values):
    mean = jnp.mean(values, axis=0, keepdims=True)
    center = values - mean
    spread = jnp.mean(center * center, axis=0, keepdims=True) + EPS
    return center * lax.rsqrt(spread), mean, jnp.sqrt(spread)


def norm_across(values):
    center = values - jnp.mean(values, axis=-1, keepdims=True)
    spread = jnp.mean(center * center, axis=-1, keepdims=True)
    return center * lax.rsqrt(spread + EPS)


def dot(a, b):
    return jnp.dot(a, b, preferred_element_type=F32)


def join_halves(a, b, half):
    first = lax.broadcasted_iota(jnp.int32, a.shape, 1) < 64
    if half == 0:
        return jnp.where(first, a, pltpu.roll(b, 64, 1))
    return jnp.where(first, pltpu.roll(a, 64, 1), b)


def window_kernel(*refs):
    inputs, (out_ref, single_out_ref), scratch = refs[:15], refs[15:17], refs[17:]
    staged, in_sems, scratch = scratch[:15], scratch[15], scratch[16:]
    (
        pair_ref,
        single_ref,
        valid_ref,
        chain_ref,
        valid_smem,
        chain_smem,
        w_tri_in_ref,
        w_tri_gate_ref,
        w_tri_out_ref,
        w_att_in_ref,
        w_att_bias_ref,
        w_att_out_ref,
        w_pair_bias_ref,
        w_single_in_ref,
        w_single_out_ref,
    ) = staged
    (
        w_in_t,
        w_gate_t,
        w_out_t,
        w_key_t,
        w_pair_slots,
        scr_a,
        scr_b,
        lr_send,
        lr_recv,
        norm_send,
        norm_recv,
        stat_send,
        stat_recv,
        prod_send,
        prod_recv,
        bias_send,
        bias_recv,
        bias_full,
        att_t_scr,
        after_scr,
        change_scr,
        query_scr,
        key_scr,
        value_scr,
        gate_scr,
        attended_scr,
        delta_send,
        delta_recv,
        pb_sum,
        pb_send,
        pb_recv,
        single_send,
        single_recv,
        single_scr,
        single_keys,
        single_values,
        lr_sems,
        norm_sems,
        stat_sems,
        prod_sems,
        bias_sems,
        bias_send_sems,
        delta_sems,
        pb_sems,
        single_sems,
    ) = scratch
    loads = [
        pltpu.make_async_copy(inputs[n], staged[n], in_sems.at[n]) for n in range(len(inputs))
    ]
    for load in loads:
        load.start()

    row, col = lax.axis_index("row"), lax.axis_index("col")
    me = row * COLS + col
    group = col * ROWS + row
    core = lax.rem(col, 2)
    partner = col + 1 - 2 * core

    barrier = pltpu.get_barrier_semaphore()

    for row_step in range(ROWS):
        for col_step in range(COLS):
            if row_step or col_step:
                pl.semaphore_signal(
                    barrier,
                    inc=1,
                    device_id=(
                        lax.rem(row + row_step, ROWS),
                        lax.rem(col + col_step, COLS),
                    ),
                    device_id_type=MESH,
                )

    for load in loads:
        load.wait()
    w_in_t[...] = jnp.transpose(w_tri_in_ref[...].astype(F32)).astype(BF16)
    w_gate_t[...] = jnp.transpose(w_tri_gate_ref[...].astype(F32)).astype(BF16)
    w_out_t[...] = jnp.transpose(w_tri_out_ref[...].astype(F32)).astype(BF16)
    lane = lax.broadcasted_iota(jnp.int32, (1, 128), 1)
    valid_pick = valid_ref[pl.ds(row // 2, 1), :].astype(F32)
    valid_row = jnp.where(
        (lane // 64) == lax.rem(row, 2), valid_pick, pltpu.roll(valid_pick, 64, 1)
    )
    for t in range(3):
        single_scr[4 * t : 4 * t + 4, :] = single_ref[:, 128 * t : 128 * t + 128].astype(F32)
    single_scr[12:16, :] = jnp.zeros((4, 128), F32)
    single_send[...] = single_scr[0:16, :].astype(BF16)

    def project_block(step, carry):
        picks = [pair_ref[pl.ds(4 * step + a, 64, stride=32), :] for a in range(4)]
        turned = jnp.transpose(jnp.concatenate(picks, axis=0))
        normed, mean, deviation = norm_down(turned)
        normed = normed.astype(BF16)
        norm_send[step] = normed
        stat_send[step] = jnp.concatenate(
            [jnp.broadcast_to(mean, (4, 256)), jnp.broadcast_to(deviation, (4, 256))], axis=0
        )
        proj = dot(w_in_t[...], normed)
        masks = []
        for s in range(2):
            at = col * 32 + 4 * step + 2 * s
            pick = jnp.where(lane < 64, valid_smem[at], valid_smem[at + 1])
            masks.append(valid_row * pick.astype(F32))
        mask = jnp.concatenate(masks, axis=1)
        left = jax.nn.sigmoid(proj[0:128]) * proj[128:256] * mask
        right = jax.nn.sigmoid(proj[256:384]) * proj[384:512] * mask
        for s in range(2):
            scr_a[pl.ds(2 * step + s, 128, stride=16), :] = left[:, s * 128 : (s + 1) * 128]
            scr_b[pl.ds(2 * step + s, 128, stride=16), :] = right[:, s * 128 : (s + 1) * 128]
        return carry

    lax.fori_loop(0, 8, project_block, 0)
    lr_send[:, 0:16, :] = scr_a[...].reshape(128, 16, 128).astype(BF16)
    lr_send[:, 16:32, :] = scr_b[...].reshape(128, 16, 128).astype(BF16)

    pl.semaphore_wait(barrier, DEVICES - 1)

    def send_lr(step, carry):
        peer = lax.rem(me + step, DEVICES)
        pltpu.make_async_remote_copy(
            src_ref=lr_send.at[peer],
            dst_ref=lr_recv.at[me],
            send_sem=lr_sems.at[0],
            recv_sem=lr_sems.at[1],
            device_id=(peer // COLS, lax.rem(peer, COLS)),
            device_id_type=MESH,
        ).start()
        return carry

    lax.fori_loop(1, DEVICES, send_lr, 0)
    lr_recv[pl.ds(me, 1)] = lr_send[pl.ds(me, 1)]

    def send_single(step, carry):
        peer = lax.rem(row + step, ROWS)
        pltpu.make_async_remote_copy(
            src_ref=single_send,
            dst_ref=single_recv.at[col // 2, core, row],
            send_sem=single_sems.at[0],
            recv_sem=single_sems.at[1],
            device_id=(peer, col),
            device_id_type=MESH,
        ).start()
        return carry

    lax.fori_loop(1, ROWS, send_single, 0)
    single_recv[col // 2, core, row] = single_send[...]

    rest = pl.ds(0, DEVICES - 1)
    pltpu.make_async_copy(lr_send.at[rest], lr_recv.at[rest], lr_sems.at[0]).wait()

    def send_norm(step, carry):
        peer = lax.rem(row + step, ROWS)
        for sent, received, sems in (
            (norm_send, norm_recv, norm_sems),
            (stat_send, stat_recv, stat_sems),
        ):
            pltpu.make_async_remote_copy(
                src_ref=sent.at[peer],
                dst_ref=received.at[row],
                send_sem=sems.at[0],
                recv_sem=sems.at[1],
                device_id=(peer, col),
                device_id_type=MESH,
            ).start()
        return carry

    lax.fori_loop(1, ROWS, send_norm, 0)
    norm_recv[pl.ds(row, 1)] = norm_send[pl.ds(row, 1)]
    stat_recv[pl.ds(row, 1)] = stat_send[pl.ds(row, 1)]

    pltpu.make_async_copy(lr_send.at[rest], lr_recv.at[rest], lr_sems.at[1]).wait()
    left_halves, right_halves = [[], []], [[], []]
    for q in range(4):
        for half in range(2):
            for halves, first in ((left_halves, 0), (right_halves, 16)):
                a = lr_recv[32 * q : 32 * q + 16, first : first + 16, :].reshape(256, 128)
                b = lr_recv[32 * q + 16 : 32 * q + 32, first : first + 16, :].reshape(256, 128)
                halves[half].append(join_halves(a.astype(F32), b.astype(F32), half))
    left_t = jnp.concatenate(
        [jnp.concatenate(left_halves[h], axis=1) for h in range(2)], axis=0
    ).astype(BF16)
    right_t = jnp.concatenate(
        [jnp.concatenate(right_halves[h], axis=1) for h in range(2)], axis=0
    )
    right_all = jnp.transpose(right_t).astype(BF16)
    product = dot(right_all, left_t)
    for ib in range(4):
        scr_a[pl.ds(ib, 512, stride=4), :] = product[:, ib * 128 : (ib + 1) * 128]
    prod_send[...] = scr_a[...].reshape(128, 16, 128).astype(BF16)

    def send_product(step, carry):
        peer = lax.rem(me + step, DEVICES)
        peer_row, peer_col = peer // COLS, lax.rem(peer, COLS)
        pltpu.make_async_remote_copy(
            src_ref=prod_send.at[peer_col * ROWS + peer_row],
            dst_ref=prod_recv.at[me],
            send_sem=prod_sems.at[0],
            recv_sem=prod_sems.at[1],
            device_id=(peer_row, peer_col),
            device_id_type=MESH,
        ).start()
        return carry

    lax.fori_loop(1, DEVICES, send_product, 0)
    prod_recv[pl.ds(me, 1)] = prod_send[pl.ds(group, 1)]

    seven = pl.ds(0, ROWS - 1)
    pltpu.make_async_copy(norm_send.at[seven], norm_recv.at[seven], norm_sems.at[1]).wait()
    pltpu.make_async_copy(stat_send.at[seven], stat_recv.at[seven], stat_sems.at[1]).wait()
    pltpu.make_async_copy(prod_send.at[rest], prod_recv.at[rest], prod_sems.at[1]).wait()

    scr_b[...] = prod_recv[...].reshape(2048, 128).astype(F32)
    valid_all = jnp.concatenate([valid_ref[a : a + 1, :] for a in range(4)], axis=1)
    key_mask = (valid_all.astype(F32) - 1.0) * 10000.0
    for jj in range(4):
        at = slice(64 * (jj // 2) * 2, 64 * (jj // 2) * 2 + 128)
        half = jj % 2
        normed = jnp.concatenate(
            [
                join_halves(
                    norm_recv[2 * ib, :, at].astype(F32),
                    norm_recv[2 * ib + 1, :, at].astype(F32),
                    half,
                )
                for ib in range(4)
            ],
            axis=1,
        )
        stats = jnp.concatenate(
            [
                join_halves(stat_recv[2 * ib, :, at], stat_recv[2 * ib + 1, :, at], half)
                for ib in range(4)
            ],
            axis=1,
        )
        received = jnp.concatenate(
            [scr_b[pl.ds(4 * jj + ib, 128, stride=16), :] for ib in range(4)], axis=1
        )
        product_norm, _, _ = norm_down(received)
        gate = jax.nn.sigmoid(dot(w_gate_t[...], normed.astype(BF16)))
        change = gate * dot(w_out_t[...], product_norm.astype(BF16))
        after = normed * stats[4:5] + stats[0:1] + change
        att_t, _, _ = norm_down(after)
        att_bf = att_t.astype(BF16)
        att_t_scr[jj] = att_bf
        after_scr[jj] = after
        change_scr[jj] = change
        bias = lax.dot_general(
            w_att_bias_ref[...], att_bf, (((1,), (0,)), ((), ())), preferred_element_type=F32
        )
        bias = bias + key_mask
        bias = (bias - jnp.max(bias, axis=1, keepdims=True)) * LOG2E
        for kb in range(4):
            scr_a[pl.ds(4 * jj + kb, 4, stride=16), :] = bias[0:4, kb * 128 : (kb + 1) * 128]
    bias_send[...] = scr_a[0:64, :].reshape(4, 16, 128).astype(BF16)

    def send_bias(slot):
        def push(step, carry):
            peer = lax.rem(me + step, DEVICES)
            pltpu.make_async_remote_copy(
                src_ref=bias_send.at[2 * lax.rem(peer, 2) + slot],
                dst_ref=bias_recv.at[slot, group],
                send_sem=bias_send_sems.at[slot],
                recv_sem=bias_sems.at[slot],
                device_id=(peer // COLS, lax.rem(peer, COLS)),
                device_id_type=MESH,
            ).start()
            return carry

        lax.fori_loop(1, DEVICES, push, 0)
        bias_recv[slot, group] = bias_send[2 * core + slot]

    def bias_left(slot):
        pltpu.make_async_copy(
            bias_recv.at[slot, rest], bias_recv.at[slot, rest], bias_send_sems.at[slot]
        ).wait()

    send_bias(0)

    w_key_t[...] = jnp.transpose(w_att_in_ref[:, 128:256].astype(F32)).astype(BF16)
    w_qvg = jnp.concatenate([w_att_in_ref[:, 0:128], w_att_in_ref[:, 256:512]], axis=1)

    for jj in range(4):
        att_bf = att_t_scr[jj]
        key_scr[jj] = dot(w_key_t[...], att_bf).astype(BF16)
        qvg = dot(jnp.transpose(att_bf.astype(F32)).astype(BF16), w_qvg)
        query_scr[jj] = (qvg[:, 0:128] * (LOG2E / math.sqrt(32.0))).astype(BF16)
        value_scr[jj, :, 0:128] = qvg[:, 128:256].astype(BF16)
        value_scr[jj, :, 128:256] = jnp.ones((512, 128), BF16)
        gate_scr[jj] = jax.nn.sigmoid(qvg[:, 256:384])
    padded = jnp.concatenate(
        [w_pair_bias_ref[...].astype(F32), jnp.zeros((112, 128), F32)], axis=0
    )
    w_pair = jnp.transpose(padded)
    for slot in range(8):
        moved = pltpu.roll(w_pair, 16 * slot, 1) if slot else w_pair
        w_pair_slots[slot] = moved.astype(BF16)
    pb_sum[...] = jnp.zeros((2, 128, 128), F32)

    across = lax.broadcasted_iota(jnp.int32, (128, 128), 1) // 32
    down = lax.broadcasted_iota(jnp.int32, (128, 512), 0) // 32

    def attend(slot, head, begins, ends):
        scr_b[...] = bias_recv[slot].reshape(2048, 128).astype(F32)
        for kb in range(4):
            bias_full[:, kb * 128 : (kb + 1) * 128] = scr_b[pl.ds(kb, 512, stride=4), :]

        for jj in range(4):
            keys = jnp.where(down == head, key_scr[jj].astype(F32), 0.0).astype(BF16)
            if ends:
                after_tok = jnp.transpose(after_scr[jj])
                change_tok = jnp.transpose(change_scr[jj])
            for ib in range(4):
                span = slice(128 * ib, 128 * ib + 128)
                scores = dot(query_scr[jj, span, :], keys) + bias_full[span, :]
                weights = jnp.exp2(scores - jnp.max(scores, axis=1, keepdims=True)).astype(BF16)
                summed = dot(weights, value_scr[jj])
                before = 0.0 if begins else attended_scr[jj, span, :]
                attended = jnp.where(across == head, summed[:, 0:128] / summed[:, 128:256], before)
                if not ends:
                    attended_scr[jj, span, :] = attended
                    continue
                tri_out = (gate_scr[jj, span, :] * attended).astype(BF16)
                added = dot(tri_out, w_att_out_ref[...])
                delta = (change_tok[span] + added).astype(BF16)
                delta_send[2 * ib, pl.ds(jj, 1)] = delta[0:64].reshape(1, 64, 128)
                delta_send[2 * ib + 1, pl.ds(jj, 1)] = delta[64:128].reshape(1, 64, 128)
                scr_a[span, :] = after_tok[span] + added
            if ends:

                def send_delta(step, carry, jj=jj):
                    peer = lax.rem(row + step, ROWS)
                    pltpu.make_async_remote_copy(
                        src_ref=delta_send.at[peer, jj],
                        dst_ref=delta_recv.at[row, jj],
                        send_sem=delta_sems.at[0],
                        recv_sem=delta_sems.at[1],
                        device_id=(peer, col),
                        device_id_type=MESH,
                    ).start()
                    return carry

                lax.fori_loop(1, ROWS, send_delta, 0)
                total = pb_sum[jj // 2]
                for a in range(4):
                    normed = norm_across(scr_a[pl.ds(a, 128, stride=4), :]).astype(BF16)
                    total = total + dot(normed, w_pair_slots[4 * (jj % 2) + a])
                pb_sum[jj // 2] = total

    def hand_on(slot):
        return pltpu.make_async_remote_copy(
            src_ref=bias_recv.at[slot],
            dst_ref=bias_recv.at[2 + slot],
            send_sem=bias_send_sems.at[2 + slot],
            recv_sem=bias_sems.at[2 + slot],
            device_id=(row, partner),
            device_id_type=MESH,
        )

    def gathered(slot):
        pltpu.make_async_copy(
            bias_recv.at[slot, rest], bias_recv.at[slot, rest], bias_sems.at[slot]
        ).wait()

    bias_left(0)
    send_bias(1)
    gathered(0)
    hand_on(0).start()
    pltpu.make_async_copy(
        single_recv.at[0, 0, seven], single_recv.at[0, 0, seven], single_sems.at[1]
    ).wait()

    def spread_single(step, carry):
        peer = lax.rem(col + 2 * step, COLS)
        pltpu.make_async_remote_copy(
            src_ref=single_recv.at[col // 2, core],
            dst_ref=single_recv.at[col // 2, core],
            send_sem=single_sems.at[2],
            recv_sem=single_sems.at[3],
            device_id=(row, peer),
            device_id_type=MESH,
        ).start()
        return carry

    lax.fori_loop(1, COLS // 2, spread_single, 0)
    attend(0, 2 * core, True, False)
    hand_on(0).wait_recv()
    attend(2, 2 * (1 - core), False, False)
    gathered(1)
    hand_on(1).start()
    pltpu.make_async_copy(
        single_recv.at[seven, 0], single_recv.at[seven, 0], single_sems.at[3]
    ).wait()
    pltpu.make_async_remote_copy(
        src_ref=single_recv.at[:, core],
        dst_ref=single_recv.at[:, core],
        send_sem=single_sems.at[4],
        recv_sem=single_sems.at[5],
        device_id=(row, partner),
        device_id_type=MESH,
    ).start()
    attend(1, 2 * core + 1, False, False)
    hand_on(1).wait_recv()
    attend(3, 2 * (1 - core) + 1, False, True)

    for u in range(2):
        pb_send[:, u, :] = pb_sum[u]

    def send_pb(step, carry):
        peer = lax.rem(me + step, DEVICES)
        pltpu.make_async_remote_copy(
            src_ref=pb_send.at[peer],
            dst_ref=pb_recv.at[group],
            send_sem=pb_sems.at[0],
            recv_sem=pb_sems.at[1],
            device_id=(peer // COLS, lax.rem(peer, COLS)),
            device_id_type=MESH,
        ).start()
        return carry

    lax.fori_loop(1, DEVICES, send_pb, 0)
    pb_recv[pl.ds(group, 1)] = pb_send[pl.ds(me, 1)]
    pltpu.make_async_copy(
        single_recv.at[:, core], single_recv.at[:, 1 - core], single_sems.at[5]
    ).wait()
    scr_b[...] = single_recv[...].reshape(2048, 128).astype(F32)
    for t in range(3):
        for a in range(4):
            for r in range(ROWS):
                single_scr[512 * t + 128 * a + 16 * r : 512 * t + 128 * a + 16 * r + 16, :] = scr_b[
                    pl.ds(16 * r + 4 * t + a, 16, stride=128), :
                ]
    single_all = jnp.concatenate(
        [single_scr[512 * t : 512 * t + 512, :] for t in range(3)], axis=1
    )
    single_norm = norm_across(single_all).astype(BF16)
    single_keys[...] = dot(single_norm, w_single_in_ref[:, 384:768]).astype(BF16)
    single_values[...] = dot(single_norm, w_single_in_ref[:, 768:1152]).astype(BF16)

    chain_all = jnp.concatenate([chain_ref[a : a + 1, :] for a in range(4)], axis=1)
    source = lax.broadcasted_iota(jnp.int32, (512, 512), 0)
    place = lax.broadcasted_iota(jnp.int32, (512, 512), 1)
    order = jnp.where(source == 4 * (place % 128) + place // 128, 1.0, 0.0).astype(BF16)
    traits = jnp.concatenate([chain_all, valid_all, jnp.zeros((6, 512), jnp.int32)], axis=0)
    ordered = dot(traits.astype(F32).astype(BF16), order)
    own = single_ref[...].astype(F32)
    own_norm = norm_across(own).astype(BF16)
    queries = dot(own_norm, w_single_in_ref[:, 0:384]).astype(BF16).astype(F32)
    gate = jax.nn.sigmoid(dot(own_norm, w_single_in_ref[:, 1152:1536]))
    head = lax.broadcasted_iota(jnp.int32, (16, 384), 0) * 24
    channel = lax.broadcasted_iota(jnp.int32, (16, 384), 1)
    mine = (channel >= head) & (channel < head + 24)
    stacked = jnp.concatenate(
        [jnp.where(mine, jnp.broadcast_to(queries[a : a + 1], (16, 384)), 0.0) for a in range(4)],
        axis=0,
    ).astype(BF16)
    scores = lax.dot_general(
        stacked, single_keys[...], (((1,), (1,)), ((), ())), preferred_element_type=F32
    ) * (1.0 / math.sqrt(24.0))
    masks = []
    for a in range(4):
        own_chain = chain_smem[4 * me + a].astype(F32)
        allowed = (ordered[0:1] == own_chain) & (ordered[1:2] == 1.0)
        masks.append(jnp.broadcast_to(jnp.where(allowed, 0.0, -10000.0), (16, 512)))

    delta_recv[pl.ds(row, 1)] = delta_send[pl.ds(row, 1)]
    pltpu.make_async_copy(delta_send.at[seven], delta_recv.at[seven], delta_sems.at[1]).wait()

    for k in range(32):
        at = pl.ds(k, 64, stride=32)
        out_ref[at, :] = pair_ref[at, :] + delta_recv[k // 4, k % 4].astype(F32)
    pltpu.make_async_copy(pb_send.at[rest], pb_recv.at[rest], pb_sems.at[1]).wait()

    turned = [jnp.transpose(pb_recv[:, u, :]) for u in range(2)]
    pair_bias = jnp.concatenate(
        [turned[jj // 2][64 * (jj % 2) : 64 * (jj % 2) + 64] for jj in range(4)], axis=1
    )
    scores = scores + pair_bias + jnp.concatenate(masks, axis=0)
    expo = jnp.exp(scores - jnp.max(scores, axis=1, keepdims=True))
    mass = jnp.sum(expo, axis=1, keepdims=True)
    summed = dot(expo.astype(BF16), single_values[...]) / mass
    attended = jnp.concatenate(
        [
            jnp.sum(jnp.where(mine, summed[16 * a : 16 * a + 16], 0.0), axis=0, keepdims=True)
            for a in range(4)
        ],
        axis=0,
    )
    single_out_ref[...] = own + dot((gate * attended).astype(BF16), w_single_out_ref[...])

    pltpu.make_async_copy(norm_send.at[seven], norm_recv.at[seven], norm_sems.at[0]).wait()
    pltpu.make_async_copy(stat_send.at[seven], stat_recv.at[seven], stat_sems.at[0]).wait()
    pltpu.make_async_copy(prod_send.at[rest], prod_recv.at[rest], prod_sems.at[0]).wait()
    bias_left(1)
    for slot in range(2):
        hand_on(slot).wait_send()
    pltpu.make_async_copy(delta_send.at[seven], delta_recv.at[seven], delta_sems.at[0]).wait()
    pltpu.make_async_copy(pb_send.at[rest], pb_recv.at[rest], pb_sems.at[0]).wait()
    pltpu.make_async_copy(
        single_recv.at[0, 0, seven], single_recv.at[0, 0, seven], single_sems.at[0]
    ).wait()
    pltpu.make_async_copy(
        single_recv.at[seven, 0], single_recv.at[seven, 0], single_sems.at[2]
    ).wait()
    pltpu.make_async_copy(
        single_recv.at[:, core], single_recv.at[:, 1 - core], single_sems.at[4]
    ).wait()


def per_device(
    pair,
    single,
    token_valid,
    chain_id,
    w_tri_in,
    w_tri_gate,
    w_tri_out,
    w_att_in,
    w_att_bias,
    w_att_out,
    w_single_in,
    w_pair_bias,
    w_single_out,
):
    vmem = pl.BlockSpec(memory_space=pltpu.VMEM)
    inputs = (
        pair.reshape(2048, 128),
        single,
        token_valid.reshape(4, 128),
        chain_id.reshape(4, 128),
        token_valid,
        chain_id,
        w_tri_in,
        w_tri_gate,
        w_tri_out,
        w_att_in,
        w_att_bias.T,
        w_att_out,
        w_pair_bias.T,
        w_single_in,
        w_single_out,
    )
    dma = pltpu.SemaphoreType.DMA
    staged = [
        pltpu.SMEM(x.shape, x.dtype) if x.ndim == 1 else pltpu.VMEM(x.shape, x.dtype)
        for x in inputs
    ]
    pair_out, single_out = pl.pallas_call(
        window_kernel,
        out_shape=(
            jax.ShapeDtypeStruct((2048, 128), F32),
            jax.ShapeDtypeStruct((4, 384), F32),
        ),
        in_specs=[pl.BlockSpec(memory_space=pltpu.HBM)] * len(inputs),
        out_specs=(vmem, vmem),
        scratch_shapes=staged
        + [
            dma((len(inputs),)),
            pltpu.VMEM((512, 128), BF16),
            pltpu.VMEM((128, 128), BF16),
            pltpu.VMEM((128, 128), BF16),
            pltpu.VMEM((128, 128), BF16),
            pltpu.VMEM((8, 128, 128), BF16),
            pltpu.VMEM((2048, 128), F32),
            pltpu.VMEM((2048, 128), F32),
            pltpu.VMEM((128, 32, 128), BF16),
            pltpu.VMEM((128, 32, 128), BF16),
            pltpu.VMEM((8, 128, 256), BF16),
            pltpu.VMEM((8, 128, 256), BF16),
            pltpu.VMEM((8, 8, 256), F32),
            pltpu.VMEM((8, 8, 256), F32),
            pltpu.VMEM((128, 16, 128), BF16),
            pltpu.VMEM((128, 16, 128), BF16),
            pltpu.VMEM((4, 16, 128), BF16),
            pltpu.VMEM((4, 128, 16, 128), BF16),
            pltpu.VMEM((512, 512), F32),
            pltpu.VMEM((4, 128, 512), BF16),
            pltpu.VMEM((4, 128, 512), F32),
            pltpu.VMEM((4, 128, 512), F32),
            pltpu.VMEM((4, 512, 128), BF16),
            pltpu.VMEM((4, 128, 512), BF16),
            pltpu.VMEM((4, 512, 256), BF16),
            pltpu.VMEM((4, 512, 128), F32),
            pltpu.VMEM((4, 512, 128), F32),
            pltpu.VMEM((8, 4, 64, 128), BF16),
            pltpu.VMEM((8, 4, 64, 128), BF16),
            pltpu.VMEM((2, 128, 128), F32),
            pltpu.VMEM((128, 2, 128), F32),
            pltpu.VMEM((128, 2, 128), F32),
            pltpu.VMEM((16, 128), BF16),
            pltpu.VMEM((8, 2, 8, 16, 128), BF16),
            pltpu.VMEM((1536, 128), F32),
            pltpu.VMEM((512, 384), BF16),
            pltpu.VMEM((512, 384), BF16),
            dma((2,)),
            dma((2,)),
            dma((2,)),
            dma((2,)),
            dma((4,)),
            dma((4,)),
            dma((2,)),
            dma((2,)),
            dma((6,)),
        ],
        compiler_params=pltpu.CompilerParams(
            collective_id=0, has_side_effects=True, vmem_limit_bytes=58 * 1024 * 1024
        ),
    )(*inputs)
    return pair_out.reshape(64, 32, 128), single_out


def solution(mesh):
    placed = (P("row", "col", None), P(("row", "col"), None)) + (P(),) * 11
    return jax.shard_map(
        per_device,
        mesh=mesh,
        in_specs=placed,
        out_specs=(P("row", "col", None), P(("row", "col"), None)),
        check_vma=False,
    )
```
